32 devices in a mesh: band: 8 (over z, y), lev: 4 (over x, core).
Axes of the slice: x: 2, y: 2, z: 4, core: 2. Of those that a mesh axis runs over, the one named last changes fastest.
Arguments:
- obs_value: float32 [32, 8, 4, 128], P(('band', 'lev')), may hold values from -6 to 6
- obs_weight: float32 [32, 8, 4, 4, 128], P(('band', 'lev')), may hold values from 0.05 to 1
- obs_row: int32 [32, 8, 4, 128], P(('band', 'lev')), may hold values from 0 to 254, as said below
- obs_lon: int32 [32, 8, 4, 128], P(('band', 'lev')), may hold values from 0 to 1439
- obs_chan: int32 [32, 8, 4, 128], P(('band', 'lev')), may hold values from 0 to 47, as said below
- obs_count: int32 [32, 8, 4], P(('band', 'lev')), may hold values from 0 to 128, as said below
- vert_cov: float32 [4, 12, 12], replicated
- variance: float32 [4, 64], replicated, may hold values from 0.2 to 2
- quad_weight: float32 [256], P('band'), may hold values from 0.5 to 2
- legendre: bfloat16 [32, 65, 256], P('band'), may hold values from -0.375 to 0.375
Outputs:
- increment: float32 [12, 4, 256, 1440], P('lev', None, 'band')
The draws below stay inside these ranges and needn't reach their ends.
Inputs may be any that keep to these rules, and one draw needn't show every extreme that they name: Every slot of bucket (s, b, q) has obs_row between b * 32 and (b + 1) * 32 - 1, and below 255. `obs_chan`: every slot of bucket (s, b, q) observes a level between q * 3 and (q + 1) * 3 - 1. `obs_count`: in every draw one destination bucket (b, q) is full from every source device; loads differ between destinations.
All inputs are finite; a program needn't handle non-finite values.
Results may differ from the reference program's by a relative error of at most 0.0003.
Values sent between devices are 32-bit elements; how exact they have to be, the bound alone decides.
A program may use at most 128 MiB of HBM per device.

```python
import math
import jax
import jax.numpy as jnp
from jax import lax

NLON = 1440
VARS = 4
LEVELS = 12
LAT_DEV = 32
CAP = 128
LEV_DEV = 3
NLAT = 256
NPAIR = 32
MORD = 64
N_BAND = 8
N_LEV = 4
DEVICES = 32


def draw_obs_row(key, part):
    key = jax.random.fold_in(key, 11)
    shape = (DEVICES, N_BAND, N_LEV, CAP)
    band_ids = lax.broadcasted_iota(jnp.int32, shape, 1)
    offset = jax.random.randint(key, shape, 0, LAT_DEV)
    return jnp.minimum(band_ids * LAT_DEV + offset, NLAT - 2).astype(jnp.int32)


def draw_obs_chan(key, part):
    key = jax.random.fold_in(key, 12)
    shape = (DEVICES, N_BAND, N_LEV, CAP)
    first_key, second_key = jax.random.split(key)
    var_ids = jax.random.randint(first_key, shape, 0, VARS)
    inner = jax.random.randint(second_key, shape, 0, LEV_DEV)
    group_ids = lax.broadcasted_iota(jnp.int32, shape, 2)
    return (var_ids * LEVELS + group_ids * LEV_DEV + inner).astype(jnp.int32)


def draw_obs_count(key, part):
    key = jax.random.fold_in(key, 13)
    shape = (DEVICES, N_BAND, N_LEV)
    first_key, second_key, third_key = jax.random.split(key, 3)
    ceiling = jax.random.randint(first_key, (1, N_BAND, N_LEV), CAP // 2, CAP + 1)
    uniform_ids = jax.random.randint(second_key, shape, 0, CAP + 1)
    counts = uniform_ids * ceiling // CAP
    chosen = jax.random.randint(third_key, (), 0, N_BAND * N_LEV)
    flat_ids = lax.broadcasted_iota(jnp.int32, shape, 1) * N_LEV + lax.broadcasted_iota(jnp.int32, shape, 2)
    return jnp.where(flat_ids == chosen, CAP, counts).astype(jnp.int32)


def draw_vert_cov(key, part):
    key = jax.random.fold_in(key, 14)
    noise = jax.random.normal(key, (VARS, LEVELS, LEVELS), jnp.float32)
    identity = jnp.eye(LEVELS, dtype=jnp.float32)[None, :, :]
    return identity + 0.2 * (noise + jnp.swapaxes(noise, 1, 2))


def with_ends(array, rng, smallest, high):
    longest = array.shape.index(max(array.shape))
    spots = []
    for shift in (0, 1):
        where = [jax.random.randint(jax.random.fold_in(rng, axis), (), 0, length) for axis, length in enumerate(array.shape)]
        where[longest] = (where[longest] + shift) % array.shape[longest]
        spots.append(tuple(where))
    return array.at[spots[0]].set(smallest).at[spots[1]].set(high)


def level_of(stream_key, dims, cuts, least, top_value):
    def one(position, shards_of):
        steps = jax.random.uniform(jax.random.fold_in(jax.random.fold_in(stream_key, 6), position), (shards_of,), jnp.float32, least / len(cuts), top_value / len(cuts))
        return jnp.repeat(jnp.exp(steps), dims[position] // shards_of).reshape((-1,) + (1,) * (len(dims) - position - 1))

    gain = one(*cuts[0])
    for cut in cuts[1:]:
        gain = gain * one(*cut)
    return gain


def gaussian(stream_key, extent, width, most, pieces=(), held_as=jnp.bfloat16):
    drawn = width * jax.random.normal(stream_key, extent, jnp.float32)
    if pieces:
        drawn = drawn * level_of(stream_key, extent, pieces, -0.22, 0.18)
    return jnp.clip(drawn, -most, most).astype(held_as)


def setup_inputs(seed: int = 0) -> dict:
    streams_of = jax.random.split(jax.random.key(seed), 11)
    return {
        "obs_value": gaussian(streams_of[0], (DEVICES, N_BAND, N_LEV, CAP), 1.0, 6.0, ((0, 32),), jnp.float32),
        "obs_weight": jnp.clip(0.05 + 0.95 * jax.random.uniform(streams_of[1], (DEVICES, N_BAND, N_LEV, 4, CAP), jnp.float32) ** level_of(streams_of[1], (DEVICES, N_BAND, N_LEV, 4, CAP), ((0, 32),), -0.2, 0.2), 0.05, 1.0),
        "obs_row": draw_obs_row(jax.random.fold_in(streams_of[10], 71), 0),
        "obs_lon": with_ends(jax.random.randint(streams_of[3], (DEVICES, N_BAND, N_LEV, CAP), 0, NLON), jax.random.fold_in(streams_of[3], 1), 0, NLON - 1).astype(jnp.int32),
        "obs_chan": draw_obs_chan(jax.random.fold_in(streams_of[10], 71), 0),
        "obs_count": draw_obs_count(jax.random.fold_in(streams_of[10], 71), 0),
        "vert_cov": draw_vert_cov(jax.random.fold_in(streams_of[10], 71), 0),
        "variance": jnp.clip(jnp.exp(jax.random.uniform(streams_of[7], (VARS, MORD), jnp.float32, math.log(0.2), math.log(2.0))), 0.2, 2.0),
        "quad_weight": jnp.clip(jnp.exp(math.log(2.0) - 1.3862944 * jax.random.uniform(streams_of[8], (NLAT,), jnp.float32) ** level_of(streams_of[8], (NLAT,), ((0, 8),), -0.2, 0.2)), 0.5, 2.0),
        "legendre": gaussian(streams_of[9], (NPAIR, MORD + 1, NLAT), NLAT ** -0.5, 0.375, ((0, 8),)),
    }


def phase_tables(orders, nlon):
    columns = jnp.arange(nlon, dtype=jnp.int32)
    phases = (orders[None, :] * columns[:, None]) % nlon
    angles = phases.astype(jnp.float32) * (2.0 * math.pi / nlon)
    return jnp.cos(angles), jnp.sin(angles)


def reference(obs_value, obs_weight, obs_row, obs_lon, obs_chan, obs_count, vert_cov, variance, quad_weight, legendre):
    highest = lax.Precision.HIGHEST
    legendre_wide = legendre.astype(jnp.float32)
    slot_ids = jnp.arange(CAP, dtype=jnp.int32)
    live_rows = slot_ids[None, None, None, :] < obs_count[..., None]
    values = jnp.where(live_rows, obs_value, jnp.float32(0.0))
    contribution = values[:, :, :, None, :] * obs_weight
    level_ids = obs_chan % LEVELS
    var_ids = obs_chan // LEVELS
    flat_channel = level_ids * VARS + var_ids
    rows_four = jnp.stack([obs_row, obs_row, obs_row + 1, obs_row + 1], axis=3)
    lons_four = jnp.stack([obs_lon, obs_lon + 1, obs_lon, obs_lon + 1], axis=3) % NLON
    targets = (flat_channel[:, :, :, None, :] * (NLAT + 1) + rows_four) * NLON + lons_four
    grad = jnp.zeros((LEVELS * VARS * (NLAT + 1) * NLON,), jnp.float32)
    grad = grad.at[targets.reshape(-1)].add(contribution.reshape(-1))
    grad = grad.reshape(LEVELS, VARS, NLAT + 1, NLON)[:, :, :NLAT]
    mixed = jnp.einsum('vkl,lvjn->kvjn', vert_cov, grad, precision=highest)
    orders = jnp.arange(MORD, dtype=jnp.int32)
    cosine_table, sine_table = phase_tables(orders, NLON)
    flat_grid = mixed.reshape(-1, NLON)
    real_part = jnp.dot(flat_grid, cosine_table, precision=highest) / NLON
    imag_part = -jnp.dot(flat_grid, sine_table, precision=highest) / NLON
    spectrum = jnp.stack([real_part, imag_part], axis=-1).reshape(LEVELS, VARS, NLAT, MORD, 2)
    weighted = spectrum * quad_weight[None, None, :, None, None]
    row_ids = jnp.arange(MORD + 1, dtype=jnp.int32)

    def per_pair(pair_id):
        lower_order = lax.dynamic_index_in_dim(weighted, pair_id, 3, keepdims=False)
        upper_order = lax.dynamic_index_in_dim(weighted, MORD - 1 - pair_id, 3, keepdims=False)
        legendre_part = lax.dynamic_index_in_dim(legendre_wide, pair_id, 0, keepdims=False)
        lower_coef = jnp.einsum('rj,kvjz->rkvz', legendre_part, lower_order, precision=highest)
        upper_coef = jnp.einsum('rj,kvjz->rkvz', legendre_part, upper_order, precision=highest)
        low_rows = row_ids < MORD - pair_id
        low_mask = low_rows[:, None, None, None]
        coefficients = jnp.where(low_mask, lower_coef, upper_coef)
        degree = jnp.where(low_rows, pair_id + row_ids, row_ids - 1)
        row_variance = jnp.take(variance, degree, axis=1).T
        scaled = coefficients * row_variance[:, None, :, None]
        lower_out = jnp.einsum('rj,rkvz->kvjz', legendre_part, jnp.where(low_mask, scaled, jnp.float32(0.0)), precision=highest)
        upper_out = jnp.einsum('rj,rkvz->kvjz', legendre_part, jnp.where(low_mask, jnp.float32(0.0), scaled), precision=highest)
        return lower_out, upper_out

    lower_all, upper_all = lax.map(per_pair, jnp.arange(NPAIR, dtype=jnp.int32))
    synthesis = jnp.concatenate([lower_all, upper_all[::-1]], axis=0)
    synthesis = jnp.moveaxis(synthesis, 0, 3)
    order_factor = jnp.where(orders == 0, jnp.float32(1.0), jnp.float32(2.0))
    flat_synth = synthesis.reshape(-1, MORD, 2)
    increment = jnp.dot(flat_synth[..., 0] * order_factor, cosine_table.T, precision=highest)
    increment = increment - jnp.dot(flat_synth[..., 1] * order_factor, sine_table.T, precision=highest)
    return increment.reshape(LEVELS, VARS, NLAT, NLON)
```

```python
import functools
import math

import jax
import jax.numpy as jnp
import ml_dtypes
import numpy as np
from jax import lax
from jax.experimental import pallas as pl
from jax.experimental.pallas import tpu as pltpu
from jax.sharding import PartitionSpec as P

NLON = 1440
FINE = 32
COARSE = 48
MESH = pl.DeviceIdType.MESH
LANES = 128
NT = (((1,), (1,)), ((), ()))
NN = (((1,), (0,)), ((), ()))


def split_np(table, parts):
    out = []
    rest = np.asarray(table, np.float64)
    for _ in range(parts):
        piece = rest.astype(np.float32).astype(ml_dtypes.bfloat16)
        out.append(piece)
        rest = rest - piece.astype(np.float64)
    return out


def row_orders(orders):
    pairs = np.arange(orders // 2)
    four = np.stack([pairs, pairs, orders - 1 - pairs, orders - 1 - pairs], axis=1).reshape(-1)
    is_sine = np.tile(np.array([0, 1, 0, 1]), orders // 2)
    return four, is_sine


def point_table(orders):
    order, is_sine = row_orders(orders)
    unit = 2.0 * math.pi / NLON
    coarse = (order[:, None] * FINE * np.arange(COARSE)[None, :] % NLON) * unit + is_sine[:, None] * (math.pi / 2)
    fine = (order[:, None] * np.arange(FINE)[None, :] % NLON) * unit
    east = (order[:, None] * (np.arange(FINE) + 1)[None, :] % NLON) * unit
    no_a, no_b = np.zeros_like(coarse), np.zeros_like(fine)
    rows = [
        np.concatenate([np.cos(coarse), no_b], 1),
        np.concatenate([np.sin(coarse), no_b], 1),
        np.concatenate([no_a, np.cos(fine)], 1),
        np.concatenate([no_a, np.sin(fine)], 1),
        np.concatenate([no_a, np.cos(east)], 1),
        np.concatenate([no_a, np.sin(east)], 1),
    ]
    parts = split_np(np.concatenate(rows, 0), 3)
    pad = np.zeros((parts[0].shape[0], 256 - 3 * (COARSE + FINE)), ml_dtypes.bfloat16)
    return np.concatenate(parts + [pad], 1)


def back_table(orders):
    order, is_sine = row_orders(orders)
    angle = (order[:, None] * np.arange(NLON)[None, :] % NLON) * (2.0 * math.pi / NLON)
    factor = np.where(order == 0, 1.0, 2.0)[:, None] / NLON
    table = factor * np.where(is_sine[:, None] == 1, -np.sin(angle), np.cos(angle))
    table = np.repeat(table.reshape(-1, 1, 4, NLON), 2, axis=1).reshape(-1, NLON)
    high, low = split_np(table, 2)
    return high, low


def observation_group(devices):
    return 4 if devices <= 64 else 1


def two(value):
    high = value.astype(jnp.bfloat16)
    low = (value - high.astype(jnp.float32)).astype(jnp.bfloat16)
    return high, low


def dot2(value, weights, dims):
    count = value.shape[0]
    both = jnp.concatenate(list(two(value)), axis=0)
    out = lax.dot_general(both, weights, dims, preferred_element_type=jnp.float32)
    return out[:count] + out[count:]


def main_kernel(
    nb, nl, levels,
    val_ref, wgt_ref, row_ref, lon_ref, chan_ref, cnt_ref, cov_ref, var_ref, quad_ref, leg_ref, tab_ref,
    out_ref,
    send1, recv1, send2, recv2, send3, recv3, acc, lpad, xbuf, ssem, rsem1, rsem2, rsem3,
):
    devices = nb * nl
    band, lev = lax.axis_index("band"), lax.axis_index("lev")
    me = band * nl + lev
    lev_local = levels // nl
    var_count = cov_ref.shape[0]
    rows2 = acc.shape[0] // 2
    orders = leg_ref.shape[1] - 1
    nj = leg_ref.shape[2]
    rp = lpad.shape[0]
    tiles = nj // LANES
    per1 = observation_group(devices)
    groups = devices // per1
    highest = lax.Precision.HIGHEST

    barrier = pltpu.get_barrier_semaphore()

    def greet(k, c):
        d = lax.rem(me + k, devices)
        pl.semaphore_signal(barrier, inc=1, device_id=(d // nl, lax.rem(d, nl)), device_id_type=MESH)
        return c

    lax.fori_loop(1, devices, greet, 0)

    slot = lax.broadcasted_iota(jnp.int32, (1, LANES), 1)

    def pack(b, c):
        for q in range(nl):
            d = b * nl + q
            live = slot < cnt_ref[b, q]
            value = jnp.where(live, val_ref[b, pl.ds(q, 1), :], 0.0)
            send1[d, 0:4, :] = value * wgt_ref[b, q]
            chan = chan_ref[b, pl.ds(q, 1), :]
            variable = jnp.where(chan >= levels, 1, 0)
            for v in range(2, var_count):
                variable = variable + jnp.where(chan >= v * levels, 1, 0)
            level = chan - variable * levels - q * lev_local
            target = (level * var_count + variable) * 32 + row_ref[b, pl.ds(q, 1), :] - b * 32
            send1[d, 4:5, :] = target.astype(jnp.float32)
            send1[d, 5:6, :] = lon_ref[b, pl.ds(q, 1), :].astype(jnp.float32)
            send1[d, 6:7, :] = quad_ref[...]
            send1[d, 7:8, :] = jnp.zeros((1, LANES), jnp.float32)
        return c

    lax.fori_loop(0, nb, pack, 0)
    pl.semaphore_wait(barrier, devices - 1)

    def scatter_out(send, recv, phase, rsem, per):
        def one(k, c):
            d = lax.rem(me + k, devices)
            pltpu.make_async_remote_copy(
                src_ref=send.at[d],
                dst_ref=recv.at[me],
                send_sem=ssem.at[phase],
                recv_sem=rsem.at[me // per],
                device_id=(d // nl, lax.rem(d, nl)),
                device_id_type=MESH,
            ).start()
            return c

        pltpu.make_async_copy(send.at[me], recv.at[me], rsem.at[me // per]).start()
        lax.fori_loop(1, devices, one, 0)

    def wait_group(recv, rsem, index, per):
        part = recv.at[pl.ds(index * per, per)]
        pltpu.make_async_copy(part, part, rsem.at[index]).wait()

    def wait_sent(send, phase):
        part = send.at[pl.ds(0, devices - 1)]
        pltpu.make_async_copy(part, part, ssem.at[phase]).wait()

    scatter_out(send1, recv1, 0, rsem1, per1)

    acc[...] = jnp.zeros_like(acc)
    lpad[...] = jnp.zeros_like(lpad)
    lpad[0:orders + 1, :] = leg_ref[lev].astype(jnp.float32)
    leg = lpad[...].astype(jnp.bfloat16)

    degree_r = lax.broadcasted_iota(jnp.int32, (orders, rp), 1)
    degree_d = lax.broadcasted_iota(jnp.int32, (orders, rp), 0)
    degree = jnp.where(degree_r < orders - me, me + degree_r, degree_r - 1)
    row_var = lax.dot_general(
        var_ref[...], jnp.where(degree == degree_d, 1.0, 0.0), NN, precision=highest, preferred_element_type=jnp.float32
    )

    per_v = nl * 16
    mr = lax.broadcasted_iota(jnp.int32, (per_v, levels), 0)
    ml = lax.broadcasted_iota(jnp.int32, (per_v, levels), 1)
    tau = (mr % 16) // 4
    expand = jnp.where((tau < lev_local) & (ml == (mr // 16) * lev_local + tau), 1.0, 0.0)
    same = lax.broadcasted_iota(jnp.int32, (per_v, per_v), 0) % 4 == lax.broadcasted_iota(jnp.int32, (per_v, per_v), 1) % 4
    mixers = []
    for v in range(var_count):
        left = lax.dot_general(expand, cov_ref[v], NN, precision=highest, preferred_element_type=jnp.float32)
        full = lax.dot_general(left, expand, NT, precision=highest, preferred_element_type=jnp.float32)
        mixers.append(jnp.where(same, full, 0.0))

    target_ids = lax.broadcasted_iota(jnp.int32, (3 * LANES, LANES), 0).astype(jnp.float32)
    coarse_ids = lax.broadcasted_iota(jnp.int32, (COARSE, LANES), 0)
    fine_ids = lax.broadcasted_iota(jnp.int32, (FINE, LANES), 0)

    def gather_obs(index, c):
        wait_group(recv1, rsem1, index, per1)
        hots, picks = [], []
        for g in range(per1):
            s = index * per1 + g
            hots.append(jnp.where(target_ids == recv1[s, 4:5, :], 1.0, 0.0).astype(jnp.bfloat16))
            lon = recv1[s, 5:6, :].astype(jnp.int32)
            a = jnp.where(coarse_ids == lon // FINE, 1.0, 0.0).astype(jnp.bfloat16)
            b = jnp.where(fine_ids == lon % FINE, 1.0, 0.0).astype(jnp.bfloat16)
            picks.append(jnp.concatenate([a, b, a, b, a, b, jnp.zeros((16, LANES), jnp.bfloat16)], axis=0))
        hot = jnp.concatenate(hots, axis=1)
        pick = jnp.concatenate(picks, axis=1)
        trig = lax.dot_general(tab_ref[...], pick, NN, preferred_element_type=jnp.float32)
        ca, sa, cb, sb, ce, se = [trig[i * rows2:(i + 1) * rows2] for i in range(6)]
        here = ca * cb - sa * sb
        east = ca * ce - sa * se
        weights = [
            jnp.concatenate([recv1[index * per1 + g, k:k + 1, :] for g in range(per1)], axis=1) for k in range(4)
        ]
        first = here * weights[0] + east * weights[1]
        second = here * weights[2] + east * weights[3]
        acc[...] += dot2(jnp.concatenate([first, second], axis=0), hot, NT)
        return c

    lax.fori_loop(0, groups, gather_obs, 0)

    lane2 = lax.broadcasted_iota(jnp.int32, (rows2, LANES), 1) % 32
    sub2 = lax.broadcasted_iota(jnp.int32, (rows2, LANES), 0) % 8
    spec = []
    halo = jnp.zeros((rows2, LANES), jnp.float32)
    for t in range(lev_local):
        columns = slice(t * LANES, (t + 1) * LANES)
        north = acc[rows2:, columns]
        spec.append(acc[0:rows2, columns] + jnp.where(lane2 >= 1, pltpu.roll(north, 1, 1), 0.0))
        halo = halo + jnp.where(lane2 == t, pltpu.roll(north, (t - 31) % LANES, 1), 0.0)
    spec.append(halo)
    for h in range(2):
        s0, s1 = spec[2 * h], spec[2 * h + 1]
        even = jnp.where(sub2 < 4, s0, pltpu.roll(s1, 4, 0)).reshape(rows2 // 8, 8, LANES)
        odd = jnp.where(sub2 < 4, pltpu.roll(s0, rows2 - 4, 0), s1).reshape(rows2 // 8, 8, LANES)
        for i in range(rows2 // 8):
            send2[2 * i, h] = even[i]
            send2[2 * i + 1, h] = odd[i]
    per2 = 4 * nl
    scatter_out(send2, recv2, 1, rsem2, per2)

    group_of = lax.broadcasted_iota(jnp.int32, (8, LANES), 1) // 32
    quads = []
    for jt in range(tiles):
        tile = jnp.zeros((8, LANES), jnp.float32)
        for beta in range(4):
            row = jnp.broadcast_to(recv1[(4 * jt + beta) * nl, 6:7, :], (8, LANES))
            tile = jnp.where(group_of == beta, row, tile)
        quads.append(tile)
    quad = jnp.concatenate(quads, axis=1)
    lane_j = lax.broadcasted_iota(jnp.int32, (8, nj), 1) % 32
    quad_next = jnp.zeros((8, nj), jnp.float32)
    for t in range(lev_local):
        quad_next = jnp.where(lane_j == t, pltpu.roll(quad, nj - 32 + t, 1), quad_next)
    lane_r = lax.broadcasted_iota(jnp.int32, (rp, nj), 1) % 32
    cross = []
    for t in range(lev_local):
        cross.append(jnp.where(lane_r == t, pltpu.roll(lpad[...], nj - 32 + t, 1), 0.0).astype(jnp.bfloat16))
    cross = jnp.concatenate(cross, axis=0)
    sub16 = lax.broadcasted_iota(jnp.int32, (per_v, LANES), 0) % 16
    lane_group = lax.broadcasted_iota(jnp.int32, (per_v, LANES), 1) // 32

    for jt in range(tiles):
        wait_group(recv2, rsem2, jt, per2)
        own = jnp.broadcast_to(quad[0:1, jt * LANES:(jt + 1) * LANES], (per_v, LANES))
        nxt = jnp.broadcast_to(quad_next[0:1, jt * LANES:(jt + 1) * LANES], (per_v, LANES))
        factor = jnp.where(sub16 >= 12, nxt, own)
        blocks = [
            recv2[(4 * jt + beta) * nl:(4 * jt + beta + 1) * nl].reshape(per_v, LANES) for beta in range(4)
        ]
        for g in range(4):
            tile = jnp.zeros((per_v, LANES), jnp.float32)
            for beta in range(4):
                turned = pltpu.roll(blocks[beta], 32 * (beta - g) % LANES, 1) if beta != g else blocks[beta]
                tile = jnp.where(lane_group == beta, turned, tile)
            xbuf[g * per_v:(g + 1) * per_v, jt * LANES:(jt + 1) * LANES] = tile * factor

    xs = xbuf[...]
    coef = dot2(xs, leg, NT)
    halves = var_count * nl
    crossing = dot2(xs.reshape(halves, 2, 8, nj)[:, 1].reshape(halves * 8, nj), cross, NT)
    c0, c1, c2 = [crossing[:, t * rp:(t + 1) * rp] for t in range(3)]
    sub_h = lax.broadcasted_iota(jnp.int32, (halves * 8, rp), 0) % 8
    up = halves * 8 - 4
    add0 = jnp.where(sub_h < 4, pltpu.roll(c0, up, 0), c1).reshape(halves, 8, rp)
    add1 = pltpu.roll(c2, up, 0).reshape(halves, 8, rp)
    r_id = lax.broadcasted_iota(jnp.int32, (1, 8, rp), 2)
    s_id = lax.broadcasted_iota(jnp.int32, (1, 8, rp), 1)
    low = r_id < orders - me
    keep0 = low == (s_id % 4 < 2)
    keep1 = keep0 & (s_id < 4)
    coef = coef.reshape(halves, 2, 8, rp)
    t0 = jnp.where(keep0, coef[:, 0] + add0, 0.0)
    t1 = jnp.where(keep1, coef[:, 1] + add1, 0.0)
    coef = jnp.stack([t0, t1], axis=1).reshape(var_count * per_v, rp)
    mixed = []
    for v in range(var_count):
        scaled = coef[v * per_v:(v + 1) * per_v] * row_var[v:v + 1]
        mixed.append(
            lax.dot_general(mixers[v], scaled, NN, precision=highest, preferred_element_type=jnp.float32)
        )
    synth = dot2(jnp.concatenate(mixed, axis=0), leg, NN)

    for jt in range(tiles):
        for beta in range(4):
            tile = jnp.zeros((per_v, LANES), jnp.float32)
            for g in range(4):
                part = synth[g * per_v:(g + 1) * per_v, jt * LANES:(jt + 1) * LANES]
                turned = pltpu.roll(part, 32 * (g - beta) % LANES, 1) if beta != g else part
                tile = jnp.where(lane_group == g, turned, tile)
            send3[(4 * jt + beta) * nl:(4 * jt + beta + 1) * nl] = tile.reshape(nl, 2, 8, LANES)
    scatter_out(send3, recv3, 2, rsem3, devices)
    wait_group(recv3, rsem3, 0, devices)
    out_ref[...] = recv3[...]
    wait_sent(send1, 0)
    wait_sent(send2, 1)
    wait_sent(send3, 2)


def back_kernel(spec_ref, high_ref, low_ref, out_ref):
    level = pl.program_id(0)
    count = spec_ref.shape[0]
    sub = lax.broadcasted_iota(jnp.int32, (count * 8, LANES), 0) % 8
    block = spec_ref[:, level // 2].reshape(count * 8, LANES)
    block = jnp.where(sub // 4 == level % 2, block, 0.0)
    high, low = two(block.T)
    both = jnp.concatenate([high, low], axis=0)
    out = lax.dot_general(both, high_ref[...], NN, preferred_element_type=jnp.float32)
    rest = lax.dot_general(high, low_ref[...], NN, preferred_element_type=jnp.float32)
    out = out[:LANES] + out[LANES:] + rest
    out_ref[...] = out.reshape(out_ref.shape)


def solution(mesh):
    nb, nl = mesh.shape["band"], mesh.shape["lev"]
    devices = nb * nl

    def body(obs_value, obs_weight, obs_row, obs_lon, obs_chan, obs_count, vert_cov, variance, quad_weight, legendre):
        var_count, levels = vert_cov.shape[:2]
        lev_local = levels // nl
        lat_rows = quad_weight.shape[0]
        pair_local, order_rows, nj = legendre.shape
        orders = order_rows - 1
        assert pair_local == nl and lat_rows == 32 and var_count == 4 and lev_local == 3
        assert orders * 2 == 4 * devices and obs_value.shape[-1] == LANES
        rp = -(-order_rows // LANES) * LANES
        vmem = pl.BlockSpec(memory_space=pltpu.VMEM)
        smem = pl.BlockSpec(memory_space=pltpu.SMEM)
        block = (devices, 2, 8, LANES)
        spec = pl.pallas_call(
            functools.partial(main_kernel, nb, nl, levels),
            out_shape=jax.ShapeDtypeStruct(block, jnp.float32),
            in_specs=[vmem] * 5 + [smem] + [vmem] * 5,
            out_specs=vmem,
            scratch_shapes=[
                pltpu.VMEM((devices, 8, LANES), jnp.float32),
                pltpu.VMEM((devices, 8, LANES), jnp.float32),
                pltpu.VMEM(block, jnp.float32),
                pltpu.VMEM(block, jnp.float32),
                pltpu.VMEM(block, jnp.float32),
                pltpu.VMEM(block, jnp.float32),
                pltpu.VMEM((4 * orders, 3 * LANES), jnp.float32),
                pltpu.VMEM((rp, nj), jnp.float32),
                pltpu.VMEM((var_count * nl * 16, nj), jnp.float32),
                pltpu.SemaphoreType.DMA((3,)),
                pltpu.SemaphoreType.DMA((devices // observation_group(devices),)),
                pltpu.SemaphoreType.DMA((nj // LANES,)),
                pltpu.SemaphoreType.DMA((1,)),
            ],
            compiler_params=pltpu.CompilerParams(
                collective_id=0, has_side_effects=True, vmem_limit_bytes=56 * 2**20
            ),
            name="spectral_covariance",
        )(
            obs_value[0], obs_weight[0], obs_row[0], obs_lon[0], obs_chan[0], obs_count[0], vert_cov, variance,
            jnp.tile(quad_weight, 4)[None], legendre, jnp.asarray(point_table(orders)),
        )
        high, low = back_table(orders)
        return pl.pallas_call(
            back_kernel,
            grid=(lev_local,),
            out_shape=jax.ShapeDtypeStruct((lev_local, var_count, lat_rows, NLON), jnp.float32),
            in_specs=[
                pl.BlockSpec(block, lambda i: (0, 0, 0, 0)),
                pl.BlockSpec(high.shape, lambda i: (0, 0)),
                pl.BlockSpec(low.shape, lambda i: (0, 0)),
            ],
            out_specs=pl.BlockSpec((1, var_count, lat_rows, NLON), lambda i: (i, 0, 0, 0)),
            compiler_params=pltpu.CompilerParams(vmem_limit_bytes=56 * 2**20),
            name="inverse_transform",
        )(spec, jnp.asarray(high), jnp.asarray(low))

    placed = (
        P(("band", "lev"), None, None, None),
        P(("band", "lev"), None, None, None, None),
        P(("band", "lev"), None, None, None),
        P(("band", "lev"), None, None, None),
        P(("band", "lev"), None, None, None),
        P(("band", "lev"), None, None),
        P(),
        P(),
        P("band"),
        P("band", None, None),
    )
    return jax.shard_map(
        body, mesh=mesh, in_specs=placed, out_specs=P("lev", None, "band", None), check_vma=False
    )
```

```python
import functools
import math

import jax
import jax.numpy as jnp
import ml_dtypes
import numpy as np
from jax import lax
from jax.experimental import pallas as pl
from jax.experimental.pallas import tpu as pltpu
from jax.sharding import PartitionSpec as P

NLON = 1440
FINE = 32
COARSE = 48
MESH = pl.DeviceIdType.MESH
LANES = 128
NT = (((1,), (1,)), ((), ()))
NN = (((1,), (0,)), ((), ()))


def split_np(table, parts):
    out = []
    rest = np.asarray(table, np.float64)
    for _ in range(parts):
        piece = rest.astype(np.float32).astype(ml_dtypes.bfloat16)
        out.append(piece)
        rest = rest - piece.astype(np.float64)
    return out


def row_orders(orders):
    pairs = np.arange(orders // 2)
    four = np.stack([pairs, pairs, orders - 1 - pairs, orders - 1 - pairs], axis=1).reshape(-1)
    is_sine = np.tile(np.array([0, 1, 0, 1]), orders // 2)
    return four, is_sine


def point_table(orders):
    order, is_sine = row_orders(orders)
    unit = 2.0 * math.pi / NLON
    coarse = (order[:, None] * FINE * np.arange(COARSE)[None, :] % NLON) * unit + is_sine[:, None] * (math.pi / 2)
    fine = (order[:, None] * np.arange(FINE)[None, :] % NLON) * unit
    east = (order[:, None] * (np.arange(FINE) + 1)[None, :] % NLON) * unit
    no_a, no_b = np.zeros_like(coarse), np.zeros_like(fine)
    rows = [
        np.concatenate([np.cos(coarse), no_b], 1),
        np.concatenate([np.sin(coarse), no_b], 1),
        np.concatenate([no_a, np.cos(fine)], 1),
        np.concatenate([no_a, np.sin(fine)], 1),
        np.concatenate([no_a, np.cos(east)], 1),
        np.concatenate([no_a, np.sin(east)], 1),
    ]
    parts = split_np(np.concatenate(rows, 0), 3)
    pad = np.zeros((parts[0].shape[0], 256 - 3 * (COARSE + FINE)), ml_dtypes.bfloat16)
    return np.concatenate(parts + [pad], 1)


def back_table(orders):
    order, is_sine = row_orders(orders)
    angle = (order[:, None] * np.arange(NLON)[None, :] % NLON) * (2.0 * math.pi / NLON)
    factor = np.where(order == 0, 1.0, 2.0)[:, None] / NLON
    table = factor * np.where(is_sine[:, None] == 1, -np.sin(angle), np.cos(angle))
    high, low = split_np(table, 2)
    return np.concatenate([high, high, low], axis=0)


def observation_group(devices):
    return 8 if devices <= 64 else 1


def two(value):
    high = value.astype(jnp.bfloat16)
    low = (value - high.astype(jnp.float32)).astype(jnp.bfloat16)
    return high, low


def dot2(value, weights, dims):
    count = value.shape[0]
    both = jnp.concatenate(list(two(value)), axis=0)
    out = lax.dot_general(both, weights, dims, preferred_element_type=jnp.float32)
    return out[:count] + out[count:]


def main_kernel(
    nb, nl, levels,
    val_ref, wgt_ref, row_ref, lon_ref, chan_ref, cnt_ref, cov_ref, var_ref, quad_ref, leg_ref, tab_ref,
    out_ref,
    send1, recv1, send2, recv2, send3, recv3, acc, lpad, xbuf, tab, quad4, tsem, ssem, rsem1, rsem2, rsem3,
):
    devices = nb * nl
    band, lev = lax.axis_index("band"), lax.axis_index("lev")
    me = band * nl + lev
    lev_local = levels // nl
    var_count = cov_ref.shape[1]
    rows2 = acc.shape[0] // 2
    turned_leg = leg_ref.shape[1] == nl
    orders = leg_ref.shape[0 if turned_leg else 1] - 1
    nj = leg_ref.shape[2]
    rp = lpad.shape[0]
    tiles = nj // LANES
    per1 = observation_group(devices)
    groups = devices // per1
    highest = lax.Precision.HIGHEST

    table_copy = pltpu.make_async_copy(tab_ref, tab, tsem)
    table_copy.start()
    barrier = pltpu.get_barrier_semaphore()

    def greet(k, c):
        d = lax.rem(me + k, devices)
        pl.semaphore_signal(barrier, inc=1, device_id=(d // nl, lax.rem(d, nl)), device_id_type=MESH)
        return c

    lax.fori_loop(1, devices, greet, 0)

    for part in range(4):
        quad4[:, part * 32:(part + 1) * 32] = quad_ref[...]

    slot = lax.broadcasted_iota(jnp.int32, (1, LANES), 1)

    def pack(b, c):
        for q in range(nl):
            d = b * nl + q
            live = slot < cnt_ref[q, b]
            value = jnp.where(live, val_ref[b, pl.ds(q, 1), :], 0.0)
            send1[d, 0:4, :] = value * wgt_ref[b, q]
            chan = chan_ref[b, pl.ds(q, 1), :]
            variable = jnp.where(chan >= levels, 1, 0)
            for v in range(2, var_count):
                variable = variable + jnp.where(chan >= v * levels, 1, 0)
            level = chan - variable * levels - q * lev_local
            target = (level * var_count + variable) * 32 + row_ref[b, pl.ds(q, 1), :] - b * 32
            send1[d, 4:5, :] = target.astype(jnp.float32)
            send1[d, 5:6, :] = lon_ref[b, pl.ds(q, 1), :].astype(jnp.float32)
            send1[d, 6:7, :] = quad4[...]
            send1[d, 7:8, :] = jnp.zeros((1, LANES), jnp.float32)
        return c

    lax.fori_loop(0, nb, pack, 0)
    pl.semaphore_wait(barrier, devices - 1)

    def scatter_out(send, recv, phase, rsem, per):
        def one(k, c):
            d = lax.rem(me + k, devices)
            pltpu.make_async_remote_copy(
                src_ref=send.at[d],
                dst_ref=recv.at[me],
                send_sem=ssem.at[phase],
                recv_sem=rsem.at[me // per],
                device_id=(d // nl, lax.rem(d, nl)),
                device_id_type=MESH,
            ).start()
            return c

        pltpu.make_async_copy(send.at[me], recv.at[me], rsem.at[me // per]).start()
        lax.fori_loop(1, devices, one, 0)

    def wait_group(recv, rsem, index, per):
        part = recv.at[pl.ds(index * per, per)]
        pltpu.make_async_copy(part, part, rsem.at[index]).wait()

    def wait_sent(send, phase):
        part = send.at[pl.ds(0, devices - 1)]
        pltpu.make_async_copy(part, part, ssem.at[phase]).wait()

    scatter_out(send1, recv1, 0, rsem1, per1)

    acc[...] = jnp.zeros_like(acc)
    lpad[...] = jnp.zeros_like(lpad)
    if turned_leg:
        wide = leg_ref[...].astype(jnp.float32)
        mine = lax.broadcasted_iota(jnp.int32, wide.shape, 1) == lev
        lpad[0:orders + 1, :] = jnp.sum(jnp.where(mine, wide, 0.0), axis=1)
    else:
        lpad[0:orders + 1, :] = leg_ref[lev].astype(jnp.float32)
    leg = lpad[...].astype(jnp.bfloat16)

    degree_r = lax.broadcasted_iota(jnp.int32, (orders, rp), 1)
    degree_d = lax.broadcasted_iota(jnp.int32, (orders, rp), 0)
    degree = jnp.where(degree_r < orders - me, me + degree_r, degree_r - 1)
    row_var = lax.dot_general(
        var_ref[...], jnp.where(degree == degree_d, 1.0, 0.0), NN, precision=highest, preferred_element_type=jnp.float32
    )

    per_v = nl * 16
    mr = lax.broadcasted_iota(jnp.int32, (per_v, levels), 0)
    ml = lax.broadcasted_iota(jnp.int32, (per_v, levels), 1)
    tau = (mr % 16) // 4
    expand = jnp.where((tau < lev_local) & (ml == (mr // 16) * lev_local + tau), 1.0, 0.0)
    same = lax.broadcasted_iota(jnp.int32, (per_v, per_v), 0) % 4 == lax.broadcasted_iota(jnp.int32, (per_v, per_v), 1) % 4
    mixers = []
    for v in range(var_count):
        left = lax.dot_general(expand, cov_ref[:, v, :], NN, precision=highest, preferred_element_type=jnp.float32)
        full = lax.dot_general(left, expand, NT, precision=highest, preferred_element_type=jnp.float32)
        mixers.append(jnp.where(same, full, 0.0))

    target_ids = lax.broadcasted_iota(jnp.int32, (3 * LANES, LANES), 0).astype(jnp.float32)
    coarse_ids = lax.broadcasted_iota(jnp.int32, (COARSE, LANES), 0)
    fine_ids = lax.broadcasted_iota(jnp.int32, (FINE, LANES), 0)

    def gather_obs(index, c):
        wait_group(recv1, rsem1, index, per1)
        hots, picks = [], []
        for g in range(per1):
            s = index * per1 + g
            hots.append(jnp.where(target_ids == recv1[s, 4:5, :], 1.0, 0.0).astype(jnp.bfloat16))
            lon = recv1[s, 5:6, :].astype(jnp.int32)
            a = jnp.where(coarse_ids == lon // FINE, 1.0, 0.0).astype(jnp.bfloat16)
            b = jnp.where(fine_ids == lon % FINE, 1.0, 0.0).astype(jnp.bfloat16)
            picks.append(jnp.concatenate([a, b, a, b, a, b, jnp.zeros((16, LANES), jnp.bfloat16)], axis=0))
        hot = jnp.concatenate(hots, axis=1)
        pick = jnp.concatenate(picks, axis=1)
        trig = lax.dot_general(tab[...], pick, NN, preferred_element_type=jnp.float32)
        ca, sa, cb, sb, ce, se = [trig[i * rows2:(i + 1) * rows2] for i in range(6)]
        here = ca * cb - sa * sb
        east = ca * ce - sa * se
        weights = [
            jnp.concatenate([recv1[index * per1 + g, k:k + 1, :] for g in range(per1)], axis=1) for k in range(4)
        ]
        first = here * weights[0] + east * weights[1]
        second = here * weights[2] + east * weights[3]
        acc[...] += dot2(jnp.concatenate([first, second], axis=0), hot, NT)
        return c

    table_copy.wait()
    lax.fori_loop(0, groups, gather_obs, 0)

    lane2 = lax.broadcasted_iota(jnp.int32, (rows2, LANES), 1) % 32
    sub2 = lax.broadcasted_iota(jnp.int32, (rows2, LANES), 0) % 8
    spec = []
    halo = jnp.zeros((rows2, LANES), jnp.float32)
    for t in range(lev_local):
        columns = slice(t * LANES, (t + 1) * LANES)
        north = acc[rows2:, columns]
        spec.append(acc[0:rows2, columns] + jnp.where(lane2 >= 1, pltpu.roll(north, 1, 1), 0.0))
        halo = halo + jnp.where(lane2 == t, pltpu.roll(north, (t - 31) % LANES, 1), 0.0)
    spec.append(halo)
    for h in range(2):
        s0, s1 = spec[2 * h], spec[2 * h + 1]
        even = jnp.where(sub2 < 4, s0, pltpu.roll(s1, 4, 0)).reshape(rows2 // 8, 8, LANES)
        odd = jnp.where(sub2 < 4, pltpu.roll(s0, rows2 - 4, 0), s1).reshape(rows2 // 8, 8, LANES)
        for i in range(rows2 // 8):
            send2[2 * i, h] = even[i]
            send2[2 * i + 1, h] = odd[i]
    per2 = 4 * nl
    scatter_out(send2, recv2, 1, rsem2, per2)

    group_of = lax.broadcasted_iota(jnp.int32, (8, LANES), 1) // 32
    quads = []
    for jt in range(tiles):
        tile = jnp.zeros((8, LANES), jnp.float32)
        for beta in range(4):
            row = jnp.broadcast_to(recv1[(4 * jt + beta) * nl, 6:7, :], (8, LANES))
            tile = jnp.where(group_of == beta, row, tile)
        quads.append(tile)
    quad = jnp.concatenate(quads, axis=1)
    lane_j = lax.broadcasted_iota(jnp.int32, (8, nj), 1) % 32
    quad_next = jnp.zeros((8, nj), jnp.float32)
    for t in range(lev_local):
        quad_next = jnp.where(lane_j == t, pltpu.roll(quad, nj - 32 + t, 1), quad_next)
    lane_r = lax.broadcasted_iota(jnp.int32, (rp, nj), 1) % 32
    cross = []
    for t in range(lev_local):
        cross.append(jnp.where(lane_r == t, pltpu.roll(lpad[...], nj - 32 + t, 1), 0.0).astype(jnp.bfloat16))
    cross = jnp.concatenate(cross, axis=0)
    sub16 = lax.broadcasted_iota(jnp.int32, (per_v, LANES), 0) % 16
    lane_group = lax.broadcasted_iota(jnp.int32, (per_v, LANES), 1) // 32

    for jt in range(tiles):
        wait_group(recv2, rsem2, jt, per2)
        own = jnp.broadcast_to(quad[0:1, jt * LANES:(jt + 1) * LANES], (per_v, LANES))
        nxt = jnp.broadcast_to(quad_next[0:1, jt * LANES:(jt + 1) * LANES], (per_v, LANES))
        factor = jnp.where(sub16 >= 12, nxt, own)
        blocks = [
            recv2[(4 * jt + beta) * nl:(4 * jt + beta + 1) * nl].reshape(per_v, LANES) for beta in range(4)
        ]
        for g in range(4):
            tile = jnp.zeros((per_v, LANES), jnp.float32)
            for beta in range(4):
                turned = pltpu.roll(blocks[beta], 32 * (beta - g) % LANES, 1) if beta != g else blocks[beta]
                tile = jnp.where(lane_group == beta, turned, tile)
            xbuf[g * per_v:(g + 1) * per_v, jt * LANES:(jt + 1) * LANES] = tile * factor

    xs = xbuf[...]
    coef = dot2(xs, leg, NT)
    halves = var_count * nl
    crossing = dot2(xs.reshape(halves, 2, 8, nj)[:, 1].reshape(halves * 8, nj), cross, NT)
    c0, c1, c2 = [crossing[:, t * rp:(t + 1) * rp] for t in range(3)]
    sub_h = lax.broadcasted_iota(jnp.int32, (halves * 8, rp), 0) % 8
    up = halves * 8 - 4
    add0 = jnp.where(sub_h < 4, pltpu.roll(c0, up, 0), c1).reshape(halves, 8, rp)
    add1 = pltpu.roll(c2, up, 0).reshape(halves, 8, rp)
    r_id = lax.broadcasted_iota(jnp.int32, (1, 8, rp), 2)
    s_id = lax.broadcasted_iota(jnp.int32, (1, 8, rp), 1)
    low = r_id < orders - me
    keep0 = low == (s_id % 4 < 2)
    keep1 = keep0 & (s_id < 4)
    coef = coef.reshape(halves, 2, 8, rp)
    t0 = jnp.where(keep0, coef[:, 0] + add0, 0.0)
    t1 = jnp.where(keep1, coef[:, 1] + add1, 0.0)
    coef = jnp.stack([t0, t1], axis=1).reshape(var_count * per_v, rp)
    mixed = []
    for v in range(var_count):
        scaled = coef[v * per_v:(v + 1) * per_v] * row_var[v:v + 1]
        mixed.append(
            lax.dot_general(mixers[v], scaled, NN, precision=highest, preferred_element_type=jnp.float32)
        )
    synth = dot2(jnp.concatenate(mixed, axis=0), leg, NN)

    for jt in range(tiles):
        for beta in range(4):
            tile = jnp.zeros((per_v, LANES), jnp.float32)
            for g in range(4):
                part = synth[g * per_v:(g + 1) * per_v, jt * LANES:(jt + 1) * LANES]
                turned = pltpu.roll(part, 32 * (g - beta) % LANES, 1) if beta != g else part
                tile = jnp.where(lane_group == g, turned, tile)
            tile = tile.reshape(nl, 2, 8, LANES)
            bands = slice((4 * jt + beta) * nl, (4 * jt + beta + 1) * nl)
            for t in range(lev_local):
                send3[bands, t] = tile[:, t // 2, 4 * (t % 2):4 * (t % 2) + 4]
    scatter_out(send3, recv3, 2, rsem3, devices)
    wait_group(recv3, rsem3, 0, devices)
    out_ref[...] = recv3[...]
    wait_sent(send1, 0)
    wait_sent(send2, 1)
    wait_sent(send3, 2)


def back_kernel(spec_ref, table_ref, out_ref, parts):
    count, lev_local = spec_ref.shape[:2]

    @pl.when(pl.program_id(0) == 0)
    def _():
        for t in range(lev_local):
            high, low = two(spec_ref[:, t].reshape(count * 4, LANES).T)
            parts[t * LANES:(t + 1) * LANES, :] = jnp.concatenate([high, low, high], axis=1)

    out = lax.dot_general(parts[...], table_ref[...], NN, preferred_element_type=jnp.float32)
    out_ref[...] = out.reshape(out_ref.shape)


def solution(mesh):
    nb, nl = mesh.shape["band"], mesh.shape["lev"]
    devices = nb * nl

    def body(obs_value, obs_weight, obs_row, obs_lon, obs_chan, obs_count, vert_cov, variance, quad_weight, legendre):
        var_count, levels = vert_cov.shape[:2]
        lev_local = levels // nl
        lat_rows = quad_weight.shape[0]
        pair_local, order_rows, nj = legendre.shape
        orders = order_rows - 1
        assert pair_local == nl and lat_rows == 32 and var_count == 4 and lev_local == 3
        assert orders * 2 == 4 * devices and obs_value.shape[-1] == LANES
        rp = -(-order_rows // LANES) * LANES
        vmem = pl.BlockSpec(memory_space=pltpu.VMEM)
        smem = pl.BlockSpec(memory_space=pltpu.SMEM)
        block = (devices, 2, 8, LANES)
        ret = (devices, lev_local, 4, LANES)
        turned_leg = orders <= 64
        spec = pl.pallas_call(
            functools.partial(main_kernel, nb, nl, levels),
            out_shape=jax.ShapeDtypeStruct(ret, jnp.float32),
            in_specs=[vmem] * 5 + [smem] + [vmem] * 4 + [pl.BlockSpec(memory_space=pl.ANY)],
            out_specs=vmem,
            scratch_shapes=[
                pltpu.VMEM((devices, 8, LANES), jnp.float32),
                pltpu.VMEM((devices, 8, LANES), jnp.float32),
                pltpu.VMEM(block, jnp.float32),
                pltpu.VMEM(block, jnp.float32),
                pltpu.VMEM(ret, jnp.float32),
                pltpu.VMEM(ret, jnp.float32),
                pltpu.VMEM((4 * orders, 3 * LANES), jnp.float32),
                pltpu.VMEM((rp, nj), jnp.float32),
                pltpu.VMEM((var_count * nl * 16, nj), jnp.float32),
                pltpu.VMEM((12 * orders, 256), jnp.bfloat16),
                pltpu.VMEM((1, LANES), jnp.float32),
                pltpu.SemaphoreType.DMA,
                pltpu.SemaphoreType.DMA((3,)),
                pltpu.SemaphoreType.DMA((devices // observation_group(devices),)),
                pltpu.SemaphoreType.DMA((nj // LANES,)),
                pltpu.SemaphoreType.DMA((1,)),
            ],
            compiler_params=pltpu.CompilerParams(
                collective_id=0, has_side_effects=True, vmem_limit_bytes=56 * 2**20
            ),
            name="spectral_covariance",
        )(
            obs_value[0], obs_weight[0], obs_row[0], obs_lon[0], obs_chan[0], obs_count[0].T, vert_cov.transpose(1, 0, 2), variance,
            quad_weight[None], legendre.transpose(1, 0, 2) if turned_leg else legendre, jnp.asarray(point_table(orders)),
        )
        table = back_table(orders)
        width = 768
        return pl.pallas_call(
            back_kernel,
            grid=(-(-NLON // width),),
            out_shape=jax.ShapeDtypeStruct((lev_local, var_count, lat_rows, NLON), jnp.float32),
            in_specs=[
                pl.BlockSpec(ret, lambda i: (0, 0, 0, 0)),
                pl.BlockSpec((table.shape[0], width), lambda i: (0, i)),
            ],
            out_specs=pl.BlockSpec((lev_local, var_count, lat_rows, width), lambda i: (0, 0, 0, i)),
            scratch_shapes=[pltpu.VMEM((lev_local * LANES, table.shape[0]), jnp.bfloat16)],
            compiler_params=pltpu.CompilerParams(vmem_limit_bytes=56 * 2**20),
            name="inverse_transform",
        )(spec, jnp.asarray(table))

    placed = (
        P(("band", "lev"), None, None, None),
        P(("band", "lev"), None, None, None, None),
        P(("band", "lev"), None, None, None),
        P(("band", "lev"), None, None, None),
        P(("band", "lev"), None, None, None),
        P(("band", "lev"), None, None),
        P(),
        P(),
        P("band"),
        P("band", None, None),
    )
    return jax.shard_map(
        body, mesh=mesh, in_specs=placed, out_specs=P("lev", None, "band", None), check_vma=False
    )
```

```python
import functools
import math

import jax
import jax.numpy as jnp
import ml_dtypes
import numpy as np
from jax import lax
from jax.experimental import pallas as pl
from jax.experimental.pallas import tpu as pltpu
from jax.sharding import PartitionSpec as P

NLON = 1440
FINE = 32
COARSE = 48
MESH = pl.DeviceIdType.MESH
LANES = 128
NT = (((1,), (1,)), ((), ()))
NN = (((1,), (0,)), ((), ()))


def split_np(table, parts):
    out = []
    rest = np.asarray(table, np.float64)
    for _ in range(parts):
        piece = rest.astype(np.float32).astype(ml_dtypes.bfloat16)
        out.append(piece)
        rest = rest - piece.astype(np.float64)
    return out


def row_orders(orders):
    pairs = np.arange(orders // 2)
    four = np.stack([pairs, pairs, orders - 1 - pairs, orders - 1 - pairs], axis=1).reshape(-1)
    is_sine = np.tile(np.array([0, 1, 0, 1]), orders // 2)
    return four, is_sine


def point_table(orders):
    order, is_sine = row_orders(orders)
    unit = 2.0 * math.pi / NLON
    coarse = (order[:, None] * FINE * np.arange(COARSE)[None, :] % NLON) * unit + is_sine[:, None] * (math.pi / 2)
    fine = (order[:, None] * np.arange(FINE)[None, :] % NLON) * unit
    east = (order[:, None] * (np.arange(FINE) + 1)[None, :] % NLON) * unit
    no_a, no_b = np.zeros_like(coarse), np.zeros_like(fine)
    rows = [
        np.concatenate([np.cos(coarse), no_b], 1),
        np.concatenate([np.sin(coarse), no_b], 1),
        np.concatenate([no_a, np.cos(fine)], 1),
        np.concatenate([no_a, np.sin(fine)], 1),
        np.concatenate([no_a, np.cos(east)], 1),
        np.concatenate([no_a, np.sin(east)], 1),
    ]
    parts = split_np(np.concatenate(rows, 0), 3)
    pad = np.zeros((parts[0].shape[0], 256 - 3 * (COARSE + FINE)), ml_dtypes.bfloat16)
    return np.concatenate(parts + [pad], 1)


def back_table(orders):
    order, is_sine = row_orders(orders)
    angle = (order[:, None] * np.arange(NLON)[None, :] % NLON) * (2.0 * math.pi / NLON)
    factor = np.where(order == 0, 1.0, 2.0)[:, None] / NLON
    table = factor * np.where(is_sine[:, None] == 1, -np.sin(angle), np.cos(angle))
    high, low = split_np(table, 2)
    return np.concatenate([high, high, low], axis=0)


def observation_group(devices):
    return 8 if devices <= 64 else 1


def two(value):
    high = value.astype(jnp.bfloat16)
    low = (value - high.astype(jnp.float32)).astype(jnp.bfloat16)
    return high, low


def dot2(value, weights, dims):
    count = value.shape[0]
    both = jnp.concatenate(list(two(value)), axis=0)
    out = lax.dot_general(both, weights, dims, preferred_element_type=jnp.float32)
    return out[:count] + out[count:]


def main_kernel(
    nb, nl, levels,
    val_ref, wgt_ref, row_ref, lon_ref, chan_ref, cnt_ref, cov_ref, var_ref, quad_ref, leg_ref, tab_ref,
    out_ref,
    send1, recv1, send2, recv2, send3, recv3, acc, lpad, xbuf, tab, quad4, tsem, ssem, rsem1, rsem2, rsem3,
):
    devices = nb * nl
    band, lev = lax.axis_index("band"), lax.axis_index("lev")
    me = band * nl + lev
    lev_local = levels // nl
    var_count = cov_ref.shape[1]
    rows2 = acc.shape[0] // 2
    turned_leg = leg_ref.shape[1] == nl
    orders = leg_ref.shape[0 if turned_leg else 1] - 1
    nj = leg_ref.shape[2]
    rp = lpad.shape[0]
    tiles = nj // LANES
    per1 = observation_group(devices)
    groups = devices // per1
    highest = lax.Precision.HIGHEST

    table_copy = pltpu.make_async_copy(tab_ref, tab, tsem)
    table_copy.start()
    barrier = pltpu.get_barrier_semaphore()

    def greet(k, c):
        d = lax.rem(me + k, devices)
        pl.semaphore_signal(barrier, inc=1, device_id=(d // nl, lax.rem(d, nl)), device_id_type=MESH)
        return c

    lax.fori_loop(1, devices, greet, 0)

    for part in range(4):
        quad4[:, part * 32:(part + 1) * 32] = quad_ref[...]

    slot = lax.broadcasted_iota(jnp.int32, (1, LANES), 1)

    def pack(b, c):
        for q in range(nl):
            d = b * nl + q
            live = slot < cnt_ref[q, b]
            value = jnp.where(live, val_ref[b, pl.ds(q, 1), :], 0.0)
            send1[d, 0:4, :] = value * wgt_ref[b, q]
            chan = chan_ref[b, pl.ds(q, 1), :]
            variable = jnp.where(chan >= levels, 1, 0)
            for v in range(2, var_count):
                variable = variable + jnp.where(chan >= v * levels, 1, 0)
            level = chan - variable * levels - q * lev_local
            target = (level * var_count + variable) * 32 + row_ref[b, pl.ds(q, 1), :] - b * 32
            send1[d, 4:5, :] = target.astype(jnp.float32)
            send1[d, 5:6, :] = lon_ref[b, pl.ds(q, 1), :].astype(jnp.float32)
            send1[d, 6:7, :] = quad4[...]
            send1[d, 7:8, :] = jnp.zeros((1, LANES), jnp.float32)
        return c

    lax.fori_loop(0, nb, pack, 0)
    pl.semaphore_wait(barrier, devices - 1)

    def scatter_out(send, recv, phase, rsem, per):
        def one(k, c):
            step = jnp.where(k % 2 == 1, (k + 1) // 2, devices - k // 2)
            d = lax.rem(me + step, devices)
            pltpu.make_async_remote_copy(
                src_ref=send.at[d],
                dst_ref=recv.at[me],
                send_sem=ssem.at[phase],
                recv_sem=rsem.at[me // per],
                device_id=(d // nl, lax.rem(d, nl)),
                device_id_type=MESH,
            ).start()
            return c

        pltpu.make_async_copy(send.at[me], recv.at[me], rsem.at[me // per]).start()
        lax.fori_loop(1, devices, one, 0, unroll=devices <= 64)

    def wait_group(recv, rsem, index, per):
        part = recv.at[pl.ds(index * per, per)]
        pltpu.make_async_copy(part, part, rsem.at[index]).wait()

    def wait_sent(send, phase):
        part = send.at[pl.ds(0, devices - 1)]
        pltpu.make_async_copy(part, part, ssem.at[phase]).wait()

    scatter_out(send1, recv1, 0, rsem1, per1)

    acc[...] = jnp.zeros_like(acc)
    lpad[...] = jnp.zeros_like(lpad)
    if turned_leg:
        wide = leg_ref[...].astype(jnp.float32)
        mine = lax.broadcasted_iota(jnp.int32, wide.shape, 1) == lev
        lpad[0:orders + 1, :] = jnp.sum(jnp.where(mine, wide, 0.0), axis=1)
    else:
        lpad[0:orders + 1, :] = leg_ref[lev].astype(jnp.float32)
    leg = lpad[...].astype(jnp.bfloat16)

    degree_r = lax.broadcasted_iota(jnp.int32, (orders, rp), 1)
    degree_d = lax.broadcasted_iota(jnp.int32, (orders, rp), 0)
    degree = jnp.where(degree_r < orders - me, me + degree_r, degree_r - 1)
    row_var = lax.dot_general(
        var_ref[...], jnp.where(degree == degree_d, 1.0, 0.0), NN, precision=highest, preferred_element_type=jnp.float32
    )

    per_v = nl * 16
    mr = lax.broadcasted_iota(jnp.int32, (per_v, levels), 0)
    ml = lax.broadcasted_iota(jnp.int32, (per_v, levels), 1)
    tau = (mr % 16) // 4
    expand = jnp.where((tau < lev_local) & (ml == (mr // 16) * lev_local + tau), 1.0, 0.0)
    same = lax.broadcasted_iota(jnp.int32, (per_v, per_v), 0) % 4 == lax.broadcasted_iota(jnp.int32, (per_v, per_v), 1) % 4
    mixers = []
    for v in range(var_count):
        left = lax.dot_general(expand, cov_ref[:, v, :], NN, precision=highest, preferred_element_type=jnp.float32)
        full = lax.dot_general(left, expand, NT, precision=highest, preferred_element_type=jnp.float32)
        mixers.append(jnp.where(same, full, 0.0))

    target_ids = lax.broadcasted_iota(jnp.int32, (3 * LANES, LANES), 0).astype(jnp.float32)
    coarse_ids = lax.broadcasted_iota(jnp.int32, (COARSE, LANES), 0)
    fine_ids = lax.broadcasted_iota(jnp.int32, (FINE, LANES), 0)

    def gather_obs(index, c):
        wait_group(recv1, rsem1, index, per1)
        hots, picks = [], []
        for g in range(per1):
            s = index * per1 + g
            hots.append(jnp.where(target_ids == recv1[s, 4:5, :], 1.0, 0.0).astype(jnp.bfloat16))
            lon = recv1[s, 5:6, :].astype(jnp.int32)
            a = jnp.where(coarse_ids == lon // FINE, 1.0, 0.0).astype(jnp.bfloat16)
            b = jnp.where(fine_ids == lon % FINE, 1.0, 0.0).astype(jnp.bfloat16)
            picks.append(jnp.concatenate([a, b, a, b, a, b, jnp.zeros((16, LANES), jnp.bfloat16)], axis=0))
        hot = jnp.concatenate(hots, axis=1)
        pick = jnp.concatenate(picks, axis=1)
        trig = lax.dot_general(tab[...], pick, NN, preferred_element_type=jnp.float32)
        ca, sa, cb, sb, ce, se = [trig[i * rows2:(i + 1) * rows2] for i in range(6)]
        here = ca * cb - sa * sb
        east = ca * ce - sa * se
        weights = [
            jnp.concatenate([recv1[index * per1 + g, k:k + 1, :] for g in range(per1)], axis=1) for k in range(4)
        ]
        first = here * weights[0] + east * weights[1]
        second = here * weights[2] + east * weights[3]
        acc[...] += dot2(jnp.concatenate([first, second], axis=0), hot, NT)
        return c

    table_copy.wait()
    lax.fori_loop(0, groups, gather_obs, 0)

    lane2 = lax.broadcasted_iota(jnp.int32, (rows2, LANES), 1) % 32
    sub2 = lax.broadcasted_iota(jnp.int32, (rows2, LANES), 0) % 8
    spec = []
    halo = jnp.zeros((rows2, LANES), jnp.float32)
    for t in range(lev_local):
        columns = slice(t * LANES, (t + 1) * LANES)
        north = acc[rows2:, columns]
        spec.append(acc[0:rows2, columns] + jnp.where(lane2 >= 1, pltpu.roll(north, 1, 1), 0.0))
        halo = halo + jnp.where(lane2 == t, pltpu.roll(north, (t - 31) % LANES, 1), 0.0)
    spec.append(halo)
    for h in range(2):
        s0, s1 = spec[2 * h], spec[2 * h + 1]
        even = jnp.where(sub2 < 4, s0, pltpu.roll(s1, 4, 0)).reshape(rows2 // 8, 8, LANES)
        odd = jnp.where(sub2 < 4, pltpu.roll(s0, rows2 - 4, 0), s1).reshape(rows2 // 8, 8, LANES)
        for i in range(rows2 // 8):
            send2[2 * i, h] = even[i]
            send2[2 * i + 1, h] = odd[i]
    per2 = 4 * nl
    scatter_out(send2, recv2, 1, rsem2, per2)

    group_of = lax.broadcasted_iota(jnp.int32, (8, LANES), 1) // 32
    quads = []
    for jt in range(tiles):
        tile = jnp.zeros((8, LANES), jnp.float32)
        for beta in range(4):
            row = jnp.broadcast_to(recv1[(4 * jt + beta) * nl, 6:7, :], (8, LANES))
            tile = jnp.where(group_of == beta, row, tile)
        quads.append(tile)
    quad = jnp.concatenate(quads, axis=1)
    lane_j = lax.broadcasted_iota(jnp.int32, (8, nj), 1) % 32
    quad_next = jnp.zeros((8, nj), jnp.float32)
    for t in range(lev_local):
        quad_next = jnp.where(lane_j == t, pltpu.roll(quad, nj - 32 + t, 1), quad_next)
    lane_r = lax.broadcasted_iota(jnp.int32, (rp, nj), 1) % 32
    cross = []
    for t in range(lev_local):
        cross.append(jnp.where(lane_r == t, pltpu.roll(lpad[...], nj - 32 + t, 1), 0.0).astype(jnp.bfloat16))
    cross = jnp.concatenate(cross, axis=0)
    sub16 = lax.broadcasted_iota(jnp.int32, (per_v, LANES), 0) % 16
    lane_group = lax.broadcasted_iota(jnp.int32, (per_v, LANES), 1) // 32

    for jt in range(tiles):
        wait_group(recv2, rsem2, jt, per2)
        own = jnp.broadcast_to(quad[0:1, jt * LANES:(jt + 1) * LANES], (per_v, LANES))
        nxt = jnp.broadcast_to(quad_next[0:1, jt * LANES:(jt + 1) * LANES], (per_v, LANES))
        factor = jnp.where(sub16 >= 12, nxt, own)
        blocks = [
            recv2[(4 * jt + beta) * nl:(4 * jt + beta + 1) * nl].reshape(per_v, LANES) for beta in range(4)
        ]
        for g in range(4):
            tile = jnp.zeros((per_v, LANES), jnp.float32)
            for beta in range(4):
                turned = pltpu.roll(blocks[beta], 32 * (beta - g) % LANES, 1) if beta != g else blocks[beta]
                tile = jnp.where(lane_group == beta, turned, tile)
            xbuf[g * per_v:(g + 1) * per_v, jt * LANES:(jt + 1) * LANES] = tile * factor

    xs = xbuf[...]
    coef = dot2(xs, leg, NT)
    halves = var_count * nl
    crossing = dot2(xs.reshape(halves, 2, 8, nj)[:, 1].reshape(halves * 8, nj), cross, NT)
    c0, c1, c2 = [crossing[:, t * rp:(t + 1) * rp] for t in range(3)]
    sub_h = lax.broadcasted_iota(jnp.int32, (halves * 8, rp), 0) % 8
    up = halves * 8 - 4
    add0 = jnp.where(sub_h < 4, pltpu.roll(c0, up, 0), c1).reshape(halves, 8, rp)
    add1 = pltpu.roll(c2, up, 0).reshape(halves, 8, rp)
    r_id = lax.broadcasted_iota(jnp.int32, (1, 8, rp), 2)
    s_id = lax.broadcasted_iota(jnp.int32, (1, 8, rp), 1)
    low = r_id < orders - me
    keep0 = low == (s_id % 4 < 2)
    keep1 = keep0 & (s_id < 4)
    coef = coef.reshape(halves, 2, 8, rp)
    t0 = jnp.where(keep0, coef[:, 0] + add0, 0.0)
    t1 = jnp.where(keep1, coef[:, 1] + add1, 0.0)
    coef = jnp.stack([t0, t1], axis=1).reshape(var_count * per_v, rp)
    mixed = []
    for v in range(var_count):
        scaled = coef[v * per_v:(v + 1) * per_v] * row_var[v:v + 1]
        mixed.append(
            lax.dot_general(mixers[v], scaled, NN, precision=highest, preferred_element_type=jnp.float32)
        )
    synth = dot2(jnp.concatenate(mixed, axis=0), leg, NN)

    for jt in range(tiles):
        for beta in range(4):
            tile = jnp.zeros((per_v, LANES), jnp.float32)
            for g in range(4):
                part = synth[g * per_v:(g + 1) * per_v, jt * LANES:(jt + 1) * LANES]
                turned = pltpu.roll(part, 32 * (g - beta) % LANES, 1) if beta != g else part
                tile = jnp.where(lane_group == g, turned, tile)
            tile = tile.reshape(nl, 2, 8, LANES)
            bands = slice((4 * jt + beta) * nl, (4 * jt + beta + 1) * nl)
            for t in range(lev_local):
                send3[bands, t] = tile[:, t // 2, 4 * (t % 2):4 * (t % 2) + 4]
    scatter_out(send3, recv3, 2, rsem3, devices)
    wait_group(recv3, rsem3, 0, devices)
    out_ref[...] = recv3[...]
    wait_sent(send1, 0)
    wait_sent(send2, 1)
    wait_sent(send3, 2)


def back_kernel(spec_ref, table_ref, out_ref, parts):
    count, lev_local = spec_ref.shape[:2]

    @pl.when(pl.program_id(0) == 0)
    def _():
        for t in range(lev_local):
            high, low = two(spec_ref[:, t].reshape(count * 4, LANES).T)
            parts[t * LANES:(t + 1) * LANES, :] = jnp.concatenate([high, low, high], axis=1)

    out = lax.dot_general(parts[...], table_ref[...], NN, preferred_element_type=jnp.float32)
    out_ref[...] = out.reshape(out_ref.shape)


def solution(mesh):
    nb, nl = mesh.shape["band"], mesh.shape["lev"]
    devices = nb * nl

    def body(obs_value, obs_weight, obs_row, obs_lon, obs_chan, obs_count, vert_cov, variance, quad_weight, legendre):
        var_count, levels = vert_cov.shape[:2]
        lev_local = levels // nl
        lat_rows = quad_weight.shape[0]
        pair_local, order_rows, nj = legendre.shape
        orders = order_rows - 1
        assert pair_local == nl and lat_rows == 32 and var_count == 4 and lev_local == 3
        assert orders * 2 == 4 * devices and obs_value.shape[-1] == LANES
        rp = -(-order_rows // LANES) * LANES
        vmem = pl.BlockSpec(memory_space=pltpu.VMEM)
        smem = pl.BlockSpec(memory_space=pltpu.SMEM)
        block = (devices, 2, 8, LANES)
        ret = (devices, lev_local, 4, LANES)
        turned_leg = orders <= 64
        spec = pl.pallas_call(
            functools.partial(main_kernel, nb, nl, levels),
            out_shape=jax.ShapeDtypeStruct(ret, jnp.float32),
            in_specs=[vmem] * 5 + [smem] + [vmem] * 4 + [pl.BlockSpec(memory_space=pl.ANY)],
            out_specs=vmem,
            scratch_shapes=[
                pltpu.VMEM((devices, 8, LANES), jnp.float32),
                pltpu.VMEM((devices, 8, LANES), jnp.float32),
                pltpu.VMEM(block, jnp.float32),
                pltpu.VMEM(block, jnp.float32),
                pltpu.VMEM(ret, jnp.float32),
                pltpu.VMEM(ret, jnp.float32),
                pltpu.VMEM((4 * orders, 3 * LANES), jnp.float32),
                pltpu.VMEM((rp, nj), jnp.float32),
                pltpu.VMEM((var_count * nl * 16, nj), jnp.float32),
                pltpu.VMEM((12 * orders, 256), jnp.bfloat16),
                pltpu.VMEM((1, LANES), jnp.float32),
                pltpu.SemaphoreType.DMA,
                pltpu.SemaphoreType.DMA((3,)),
                pltpu.SemaphoreType.DMA((devices // observation_group(devices),)),
                pltpu.SemaphoreType.DMA((nj // LANES,)),
                pltpu.SemaphoreType.DMA((1,)),
            ],
            compiler_params=pltpu.CompilerParams(
                collective_id=0, has_side_effects=True, vmem_limit_bytes=56 * 2**20
            ),
            name="spectral_covariance",
        )(
            obs_value[0], obs_weight[0], obs_row[0], obs_lon[0], obs_chan[0], obs_count[0].T, vert_cov.transpose(1, 0, 2), variance,
            quad_weight[None], legendre.transpose(1, 0, 2) if turned_leg else legendre, jnp.asarray(point_table(orders)),
        )
        table = back_table(orders)
        width = 768
        return pl.pallas_call(
            back_kernel,
            grid=(-(-NLON // width),),
            out_shape=jax.ShapeDtypeStruct((lev_local, var_count, lat_rows, NLON), jnp.float32),
            in_specs=[
                pl.BlockSpec(ret, lambda i: (0, 0, 0, 0)),
                pl.BlockSpec((table.shape[0], width), lambda i: (0, i)),
            ],
            out_specs=pl.BlockSpec((lev_local, var_count, lat_rows, width), lambda i: (0, 0, 0, i)),
            scratch_shapes=[pltpu.VMEM((lev_local * LANES, table.shape[0]), jnp.bfloat16)],
            compiler_params=pltpu.CompilerParams(vmem_limit_bytes=56 * 2**20),
            name="inverse_transform",
        )(spec, jnp.asarray(table))

    placed = (
        P(("band", "lev"), None, None, None),
        P(("band", "lev"), None, None, None, None),
        P(("band", "lev"), None, None, None),
        P(("band", "lev"), None, None, None),
        P(("band", "lev"), None, None, None),
        P(("band", "lev"), None, None),
        P(),
        P(),
        P("band"),
        P("band", None, None),
    )
    return jax.shard_map(
        body, mesh=mesh, in_specs=placed, out_specs=P("lev", None, "band", None), check_vma=False
    )
```
